32 devices in a mesh: groups: 2 (over y), wide: 8 (over z, x), short: 2 (over core).
Axes of the slice: x: 2, y: 2, z: 4, core: 2. Of those that a mesh axis runs over, the one named last changes fastest.
Arguments:
- tokens: bfloat16 [64, 5120], P(('groups', 'wide'), 'short'), parts along dimension 0, may hold values from -6 to 6
- norm_gain: float32 [5120], P('short'), may hold values from 0.5 to 1.5
- mixer_in: bfloat16 [5120, 2, 5888], P('short', None, 'wide'), may hold values from -0.078125 to 0.078125
- shared_in: bfloat16 [5120, 512], P('short', 'wide'), may hold values from -0.078125 to 0.078125
- step_in: bfloat16 [5120, 32], P('short'), may hold values from -0.078125 to 0.078125
- step_bias: float32 [32], P('short'), may hold values from -2 to 1
- decay_rate: float32 [32], P('short'), may hold values from 0.05 to 4
- skip_gain: float32 [32], P('short'), may hold values from 0.2 to 1.5
- cached_keys: bfloat16 [16, 512, 512], P(('groups', 'wide'), None, 'short'), parts along dimension 0, may hold values from -64 to 64
- cached_values: bfloat16 [16, 512, 512], P(('groups', 'wide'), None, 'short'), parts along dimension 0, may hold values from -6 to 6
- lengths: int32 [16], P(('groups', 'wide')), parts along dimension 0, may hold values from 2 to 512, as said below
- state_cache: bfloat16 [16, 32, 128, 256], P(('groups', 'wide'), 'short'), parts along dimension 0, may hold values from -6 to 6
- mixer_gain: float32 [4096], P('short'), may hold values from 0.5 to 1.5
- mixer_out: bfloat16 [2, 3328, 5120], P(None, 'wide', 'short'), may hold values from -0.078125 to 0.078125
- gate_weight: bfloat16 [5120, 21504], P('short', 'wide'), may hold values from -0.078125 to 0.078125
- up_weight: bfloat16 [5120, 21504], P('short', 'wide'), may hold values from -0.078125 to 0.078125
- down_weight: bfloat16 [21504, 5120], P('wide', 'short'), may hold values from -0.0390625 to 0.0390625
Outputs:
- mixed: bfloat16 [64, 5120], P(('groups', 'wide'), 'short'), parts along dimension 0
The draws below stay inside these ranges and needn't reach their ends.
There are 2 independent parts, one for each index of `groups`. The reference program is written for one: setup_inputs(seed, part) draws one part's arguments, and reference() takes and returns one part's arrays. A program takes and returns all parts, laid end to end along the dimension named above; an argument that names none is the same for every part. Nothing has to cross between parts.
Inputs may be any that keep to these rules, and one draw needn't show every extreme that they name: `lengths`: in every draw some request holds exactly 512 earlier tokens.
All inputs are finite; a program needn't handle non-finite values.
Results may differ from the reference program's by a relative error of at most 0.009.
Values may be sent and summed in bfloat16 or wider, within the bound.
No kernel may reach another device: no remote copies, remote signals or barrier semaphores. Data moves between devices by JAX's collectives and lax.ppermute only.
A program may use at most 128 MiB of HBM per device.

```python
import math
import jax
import jax.numpy as jnp
from jax import lax

D = 5120
QUERY_HEADS = 20
KEY_VALUE_HEADS = 4
HEAD_SIZE = 128
MH = 32
MP = 128
NS = 256
FF = 21504
CACHE_SLOTS = 512
DRAFT_TOKENS = 4
HEAD_GROUPS = 2
REQUEST_COUNT = 8
ROWS = 32
GCOL = 5888
OCOL = 3328


def draw_lengths(key, part):
    drawn = jax.random.randint(key, (REQUEST_COUNT,), 2, CACHE_SLOTS + 1)
    chosen = jax.random.randint(jax.random.fold_in(key, 11), (), 0, REQUEST_COUNT)
    return jnp.where(jnp.arange(REQUEST_COUNT) == chosen, CACHE_SLOTS, drawn).astype(jnp.int32)


def draw_cached_keys(key, part):
    cache_entries = jax.random.normal(key, (REQUEST_COUNT, CACHE_SLOTS, KEY_VALUE_HEADS * HEAD_SIZE), jnp.float32)
    return jnp.clip(cache_entries, -64.0, 64.0).astype(jnp.bfloat16)


def block_levels(key, extent, shards, smallest, top_value):
    def one(axis_at, blocks):
        draws = jax.random.uniform(jax.random.fold_in(jax.random.fold_in(key, 6), axis_at), (blocks,), jnp.float32, smallest / len(shards), top_value / len(shards))
        return jnp.repeat(jnp.exp(draws), extent[axis_at] // blocks).reshape((-1,) + (1,) * (len(extent) - axis_at - 1))

    level = one(*shards[0])
    for cut in shards[1:]:
        level = level * one(*cut)
    return level


def normal_values(key, shape, spread, bound, cuts=(), kind=jnp.bfloat16):
    result = jax.random.normal(key, shape, jnp.float32) * spread
    if len(cuts) > 0:
        result = block_levels(key, shape, cuts, -0.22, 0.18) * result
    return jnp.clip(result, min=-bound, max=bound).astype(kind)


def setup_inputs(seed: int = 0, part: int = 0) -> dict:
    key_list = jax.random.split(jax.random.key(seed), 18)
    part_splits = jax.random.split(jax.random.fold_in(key_list[17], part), 18)
    return {
        "tokens": normal_values(part_splits[0], (ROWS, D), 1.0, 6.0, ((0, 8), (1, 2))),
        "norm_gain": jnp.clip(1.0 + 0.1 * jax.random.normal(key_list[1], (D,), jnp.float32), 0.5, 1.5),
        "mixer_in": normal_values(key_list[2], (D, HEAD_GROUPS, GCOL), D ** -0.5, 0.078125, ((0, 2), (2, 8))),
        "shared_in": normal_values(key_list[3], (D, 2 * NS), D ** -0.5, 0.078125, ((0, 2), (1, 8))),
        "step_in": normal_values(key_list[4], (D, MH), D ** -0.5, 0.078125, ((0, 2),)),
        "step_bias": jnp.clip(-2.0 + 3.0 * jax.random.uniform(key_list[5], (MH,), jnp.float32) ** block_levels(key_list[5], (MH,), ((0, 2),), -0.2, 0.2), -2.0, 1.0),
        "decay_rate": jnp.clip(jnp.exp(math.log(4.0) - 4.3820266 * jax.random.uniform(key_list[6], (MH,), jnp.float32) ** block_levels(key_list[6], (MH,), ((0, 2),), -0.2, 0.2)), 0.05, 4.0),
        "skip_gain": jnp.clip(0.2 + 1.3 * jax.random.uniform(key_list[7], (MH,), jnp.float32) ** block_levels(key_list[7], (MH,), ((0, 2),), -0.2, 0.2), 0.2, 1.5),
        "cached_keys": draw_cached_keys(jax.random.fold_in(jax.random.fold_in(key_list[17], part), 71), part),
        "cached_values": normal_values(part_splits[9], (REQUEST_COUNT, CACHE_SLOTS, KEY_VALUE_HEADS * HEAD_SIZE), 1.0, 6.0, ((0, 8), (2, 2))),
        "lengths": draw_lengths(jax.random.fold_in(jax.random.fold_in(key_list[17], part), 71), part),
        "state_cache": normal_values(part_splits[11], (REQUEST_COUNT, MH, MP, NS), 1.0, 6.0, ((0, 8), (1, 2))),
        "mixer_gain": jnp.clip(1.0 + 0.1 * jax.random.normal(key_list[12], (MH * MP,), jnp.float32), 0.5, 1.5),
        "mixer_out": normal_values(key_list[13], (HEAD_GROUPS, OCOL, D), (HEAD_GROUPS * OCOL) ** -0.5, 0.078125, ((1, 8), (2, 2))),
        "gate_weight": normal_values(key_list[14], (D, FF), D ** -0.5, 0.078125, ((0, 2), (1, 8))),
        "up_weight": normal_values(key_list[15], (D, FF), D ** -0.5, 0.078125, ((0, 2), (1, 8))),
        "down_weight": normal_values(key_list[16], (FF, D), FF ** -0.5, 0.0390625, ((0, 8), (1, 2))),
    }


epsilon = 1e-05

def rotate(vectors, cos_table, sin_table):
    half_width = vectors.shape[-1] // 2
    first_half = vectors[..., :half_width]
    second_half = vectors[..., half_width:]
    return jnp.concatenate([first_half * cos_table - second_half * sin_table, second_half * cos_table + first_half * sin_table], axis=-1)

def rope_tables(positions):
    frequency = 10000.0 ** (-(jnp.arange(HEAD_SIZE // 2, dtype=jnp.float32) * 2.0 / HEAD_SIZE))
    angles = positions.astype(jnp.float32)[..., None] * frequency
    return (jnp.cos(angles), jnp.sin(angles))

def attend_one(packed):
    queries, fresh_keys, fresh_values, key_tile_block, value_tile_block, length = packed
    score_scale = HEAD_SIZE ** (-0.5)
    query_float = queries.astype(jnp.float32)
    scores_cache = jnp.einsum('tkgd,pkd->kgtp', query_float, key_tile_block.astype(jnp.float32)) * score_scale
    scores_new = jnp.einsum('tkgd,ukd->kgtu', query_float, fresh_keys.astype(jnp.float32)) * score_scale
    live_keys = jnp.arange(key_tile_block.shape[0], dtype=jnp.int32) < length
    causal = jnp.arange(DRAFT_TOKENS)[None, :] <= jnp.arange(DRAFT_TOKENS)[:, None]
    scores_cache = jnp.where(live_keys, scores_cache, -1e+30)
    scores_new = jnp.where(causal, scores_new, -1e+30)
    highest = jnp.maximum(lax.optimization_barrier(jnp.max(scores_cache, axis=-1)), lax.optimization_barrier(jnp.max(scores_new, axis=-1)))[..., None]
    weight_cache = jnp.exp(scores_cache - highest)
    weight_new = jnp.exp(scores_new - highest)
    denominator = lax.optimization_barrier(jnp.sum(weight_cache, axis=-1, keepdims=True)) + lax.optimization_barrier(jnp.sum(weight_new, axis=-1, keepdims=True))
    probs_cache = (weight_cache / denominator).astype(jnp.bfloat16)
    probs_new = (weight_new / denominator).astype(jnp.bfloat16)
    attended = jnp.einsum('kgtp,pkd->tkgd', probs_cache.astype(jnp.float32), value_tile_block.astype(jnp.float32))
    attended = attended + jnp.einsum('kgtu,ukd->tkgd', probs_new.astype(jnp.float32), fresh_values.astype(jnp.float32))
    return attended.astype(jnp.bfloat16)

def scan_one(state_block, inputs_x, gates_z, b_vals, c_vals, step_sizes, decay_rates, skip_gain, head_gain):
    hstate = state_block.astype(jnp.float32)
    in_active = jax.nn.silu(inputs_x.astype(jnp.float32))
    write_vec = jax.nn.silu(b_vals.astype(jnp.float32))
    read_vec = jax.nn.silu(c_vals.astype(jnp.float32))
    outputs = []
    for draft_index in range(DRAFT_TOKENS):
        decays = jnp.exp(-step_sizes[draft_index] * decay_rates)
        inject = (step_sizes[draft_index][:, None] * in_active[draft_index])[:, :, None] * write_vec[draft_index][None, None, :]
        hstate = decays[:, None, None] * hstate + inject
        readout = jnp.einsum('hpn,n->hp', hstate, read_vec[draft_index], precision=lax.Precision.HIGHEST)
        outputs.append(readout + skip_gain[:, None] * in_active[draft_index])
    gated = jnp.stack(outputs) * jax.nn.silu(gates_z.astype(jnp.float32))
    mean_square = lax.optimization_barrier(jnp.mean(gated * gated, axis=-1, keepdims=True))
    return (gated * lax.rsqrt(mean_square + epsilon) * head_gain).astype(jnp.bfloat16)

def reference(tokens, norm_gain, mixer_in, shared_in, step_in, step_bias, decay_rate, skip_gain, cached_keys, cached_values, lengths, state_cache, mixer_gain, mixer_out, gate_weight, up_weight, down_weight):
    q_heads = QUERY_HEADS // HEAD_GROUPS
    key_value_heads = KEY_VALUE_HEADS // HEAD_GROUPS
    ssm_heads = MH // HEAD_GROUPS
    repeat_factor = QUERY_HEADS // KEY_VALUE_HEADS
    query_size = q_heads * HEAD_SIZE
    key_size = key_value_heads * HEAD_SIZE
    m_size = ssm_heads * MP
    rows_float = tokens.astype(jnp.float32)
    inv_rms = lax.rsqrt(lax.optimization_barrier(jnp.mean(rows_float * rows_float, axis=1, keepdims=True)) + epsilon)
    normed = (rows_float * inv_rms * norm_gain[None, :]).astype(jnp.bfloat16)
    grouped_heads = jnp.dot(normed, mixer_in.reshape(D, HEAD_GROUPS * GCOL), preferred_element_type=jnp.float32).astype(jnp.bfloat16)
    grouped_heads = grouped_heads.reshape(ROWS, HEAD_GROUPS, GCOL)
    shared = jnp.dot(normed, shared_in, preferred_element_type=jnp.float32).astype(jnp.bfloat16)
    step_raw = jnp.dot(normed, step_in, preferred_element_type=jnp.float32)
    gate_sum = jnp.dot(normed, gate_weight, preferred_element_type=jnp.float32)
    up_sum = jnp.dot(normed, up_weight, preferred_element_type=jnp.float32)
    hidden = (jax.nn.silu(gate_sum) * up_sum).astype(jnp.bfloat16)
    queries = grouped_heads[:, :, :query_size].reshape(REQUEST_COUNT, DRAFT_TOKENS, QUERY_HEADS, HEAD_SIZE)
    fresh_keys = grouped_heads[:, :, query_size:query_size + key_size].reshape(REQUEST_COUNT, DRAFT_TOKENS, KEY_VALUE_HEADS, HEAD_SIZE)
    fresh_values = grouped_heads[:, :, query_size + key_size:query_size + 2 * key_size].reshape(REQUEST_COUNT, DRAFT_TOKENS, KEY_VALUE_HEADS, HEAD_SIZE)
    x_start = query_size + 2 * key_size
    inputs_x = grouped_heads[:, :, x_start:x_start + m_size].reshape(REQUEST_COUNT, DRAFT_TOKENS, MH, MP)
    gates_z = grouped_heads[:, :, x_start + m_size:x_start + 2 * m_size].reshape(REQUEST_COUNT, DRAFT_TOKENS, MH, MP)
    positions = lengths[:, None] + jnp.arange(DRAFT_TOKENS, dtype=jnp.int32)[None, :]
    cos_table, sin_table = rope_tables(positions)
    cos_table = cos_table[:, :, None, :]
    sin_table = sin_table[:, :, None, :]
    rotated_queries = rotate(queries.astype(jnp.float32), cos_table, sin_table).astype(jnp.bfloat16)
    keys_rot = rotate(fresh_keys.astype(jnp.float32), cos_table, sin_table).astype(jnp.bfloat16)
    rotated_queries = rotated_queries.reshape(REQUEST_COUNT, DRAFT_TOKENS, KEY_VALUE_HEADS, repeat_factor, HEAD_SIZE)
    key_tile_block = cached_keys.reshape(REQUEST_COUNT, CACHE_SLOTS, KEY_VALUE_HEADS, HEAD_SIZE)
    value_tile_block = cached_values.reshape(REQUEST_COUNT, CACHE_SLOTS, KEY_VALUE_HEADS, HEAD_SIZE)
    attention = lax.map(attend_one, (rotated_queries, keys_rot, fresh_values, key_tile_block, value_tile_block, lengths))
    step_sizes = jax.nn.softplus(step_raw.reshape(REQUEST_COUNT, DRAFT_TOKENS, MH) + step_bias[None, None, :])
    b_vals = shared[:, :NS].reshape(REQUEST_COUNT, DRAFT_TOKENS, NS)
    c_vals = shared[:, NS:].reshape(REQUEST_COUNT, DRAFT_TOKENS, NS)
    head_gain = mixer_gain.reshape(MH, MP)

    def mamba_one(packed):
        return scan_one(packed[0], packed[1], packed[2], packed[3], packed[4], packed[5], decay_rate, skip_gain, head_gain)
    mamba = lax.map(mamba_one, (state_cache, inputs_x, gates_z, b_vals, c_vals, step_sizes))
    mixer_rows = jnp.concatenate([attention.reshape(ROWS, HEAD_GROUPS, query_size), mamba.reshape(ROWS, HEAD_GROUPS, m_size)], axis=2)
    summed = jnp.dot(mixer_rows.reshape(ROWS, HEAD_GROUPS * OCOL), mixer_out.reshape(HEAD_GROUPS * OCOL, D), preferred_element_type=jnp.float32)
    summed = summed + jnp.dot(hidden, down_weight, preferred_element_type=jnp.float32)
    return (rows_float + summed).astype(jnp.bfloat16)
```

```python
import functools

import jax
import jax.numpy as jnp
from jax import lax
from jax.experimental import pallas as pl
from jax.experimental.pallas import tpu as pltpu
from jax.sharding import PartitionSpec as P

QUERY_HEADS = 20
KEY_VALUE_HEADS = 4
HEAD_SIZE = 128
DRAFT_TOKENS = 4

epsilon = 1e-05
LANES = 128
MIB = 2**20
F32 = jnp.float32
BF16 = jnp.bfloat16

IN_VMEM = pl.BlockSpec(memory_space=pltpu.VMEM)
IN_SMEM = pl.BlockSpec(memory_space=pltpu.SMEM)
ANYWHERE = pl.BlockSpec(memory_space=pl.ANY)


def round_up(n, m):
    return -(-n // m) * m


def silu(v):
    return v / (1.0 + jnp.exp(-v))


def dot_nt(a, b):
    return lax.dot_general(a, b, (((1,), (1,)), ((), ())), preferred_element_type=F32)


def dot_nn(a, b):
    return jnp.dot(a, b, preferred_element_type=F32)


def call(body, out_shape, args, specs, scratch=(), limit=16, flops=0, nbytes=0, name=None):
    outs = jax.tree.map(lambda _: IN_VMEM, out_shape)
    return pl.pallas_call(
        body,
        out_shape=out_shape,
        in_specs=specs,
        out_specs=outs,
        scratch_shapes=list(scratch),
        compiler_params=pltpu.CompilerParams(vmem_limit_bytes=limit * MIB),
        cost_estimate=pl.CostEstimate(flops=flops, bytes_accessed=nbytes, transcendentals=0),
        name=name,
    )(*args)


def project_body(order, place, x_ref, gain_ref, wm_ref, ws_ref, wt_ref, xg_ref, keep_ref, send_ref, xs):
    wide_at = place[0]
    mine = place[1]
    for i, rel in enumerate(order):
        xs[wide_at ^ rel] = x_ref[i].astype(F32)
    blocks, rows, width = xs.shape
    x = xs[...].reshape(blocks * rows, width)
    squares = jnp.sum(x * x, axis=1, keepdims=True)
    xg = (x * gain_ref[...]).astype(BF16)
    xg_ref[...] = xg
    columns = wm_ref.shape[1]
    padded = round_up(columns, LANES)
    shared = ws_ref.shape[0]
    shared_at = padded
    step_at = shared_at + round_up(shared, LANES)
    square_at = step_at + LANES
    heads = wt_ref.shape[1]
    both = dot_nt(xg, ws_ref[...])
    for ref, group in ((send_ref, 1 - mine), (keep_ref, mine)):
        ref[:, :columns] = dot_nt(xg, wm_ref[group])
        ref[:, shared_at : shared_at + shared] = both
        ref[:, step_at : step_at + heads] = dot_nt(xg, wt_ref[group])
        ref[:, square_at : square_at + LANES] = jnp.broadcast_to(squares, (blocks * rows, LANES))


def combine_body(width, heads, place, keep_ref, recv_ref, feat_ref, inv_ref, step_ref, ss):
    wide_at = place[0]
    blocks, rows, used = feat_ref.shape
    step_at = used
    square_at = step_at + LANES
    mean = (keep_ref[:, square_at:] + recv_ref[:, square_at:]) / width
    inv = lax.rsqrt(mean + epsilon)
    inv_ref[...] = inv
    feat = (keep_ref[:, :used] + recv_ref[:, :used]) * inv[:, :1]
    feat_ref[...] = feat.reshape(blocks, rows, used).astype(BF16)
    step = (keep_ref[:, step_at:square_at] + recv_ref[:, step_at:square_at]) * inv
    ss[...] = step.reshape(blocks, rows, LANES)
    step_ref[...] = ss[wide_at]


def mixer_body(
    dims,
    length_ref,
    feat_ref,
    step_ref,
    cos_ref,
    sin_ref,
    bias_ref,
    decay_ref,
    skip_ref,
    gain_ref,
    key_ref,
    value_ref,
    state_ref,
    out_ref,
    fs,
    bc,
    own,
):
    columns, shared, shared_at, q_heads, kv_heads, heads, head_width = dims
    t_count = DRAFT_TOKENS
    hs = HEAD_SIZE
    repeat = q_heads // kv_heads
    sources = feat_ref.shape[0]
    for i in range(sources):
        fs[:, i * columns : (i + 1) * columns] = feat_ref[i, :, :columns].astype(F32)
        bc[:, i * shared : (i + 1) * shared] = feat_ref[i, :, shared_at : shared_at + shared].astype(F32)
    length = length_ref[0]

    turned = q_heads + kv_heads
    stacked = jnp.concatenate([fs[:, h * hs : (h + 1) * hs] for h in range(turned)], axis=0)
    cos = jnp.concatenate([cos_ref[...]] * turned, axis=0)
    sin = jnp.concatenate([sin_ref[...]] * turned, axis=0)
    swapped = jnp.concatenate([stacked[:, hs // 2 :], stacked[:, : hs // 2]], axis=1)
    rotated = stacked * cos + swapped * sin
    slots = key_ref.shape[0]
    scale = hs ** (-0.5)
    group_rows = repeat * t_count
    live = lax.broadcasted_iota(jnp.int32, (group_rows, slots), 1) < length
    row_t = lax.broadcasted_iota(jnp.int32, (group_rows, LANES), 0) % t_count
    causal = lax.broadcasted_iota(jnp.int32, (group_rows, LANES), 1) <= row_t
    filler = jnp.zeros((LANES - t_count, hs), F32)
    for k in range(kv_heads):
        queries = rotated[k * group_rows : (k + 1) * group_rows].astype(BF16)
        at = q_heads * t_count + k * t_count
        new_keys = jnp.concatenate([rotated[at : at + t_count], filler], axis=0).astype(BF16)
        v_at = (turned + k) * hs
        new_values = jnp.concatenate([fs[:, v_at : v_at + hs], filler], axis=0).astype(BF16)
        head = slice(k * hs, (k + 1) * hs)
        cache = jnp.where(live, dot_nt(queries, key_ref[:, head]) * scale, -1e30)
        fresh = jnp.where(causal, dot_nt(queries, new_keys) * scale, -1e30)
        highest = jnp.maximum(
            jnp.max(cache, axis=1, keepdims=True), jnp.max(fresh, axis=1, keepdims=True)
        )
        cache = jnp.exp(cache - highest)
        fresh = jnp.exp(fresh - highest)
        total = jnp.sum(cache, axis=1, keepdims=True) + jnp.sum(fresh, axis=1, keepdims=True)
        attended = dot_nn((cache / total).astype(BF16), value_ref[:, head]) + dot_nn(
            (fresh / total).astype(BF16), new_values
        )
        for r in range(repeat):
            h = k * repeat + r
            own[:, h * hs : (h + 1) * hs] = attended[r * t_count : (r + 1) * t_count]

    x_at = (turned + kv_heads) * hs
    m_size = heads * head_width
    states = bc.shape[1] // 2
    x = silu(fs[:, x_at : x_at + m_size])
    gate = silu(fs[:, x_at + m_size : x_at + 2 * m_size])
    write = silu(bc[:, :states])
    read = silu(bc[:, states:])
    read_high = read.astype(BF16)
    read_low = (read - read_high.astype(F32)).astype(BF16)
    carried = dot_nt(read_high, state_ref[...]) + dot_nt(read_low, state_ref[...])
    raw = step_ref[:, :heads] + bias_ref[...]
    step = jnp.maximum(raw, 0.0) + jnp.log1p(jnp.exp(-jnp.abs(raw)))
    rate = -step * decay_ref[...]
    sums = [rate[0:1]]
    for t in range(1, t_count):
        sums.append(sums[-1] + rate[t : t + 1])
    sums = jnp.concatenate(sums, axis=0)

    def spread(v):
        return jnp.concatenate(
            [jnp.broadcast_to(v[:, h : h + 1], (v.shape[0], head_width)) for h in range(heads)], axis=1
        )

    sums = spread(sums)
    pushed = spread(step) * x
    skip = spread(skip_ref[...])
    readout = []
    for t in range(t_count):
        row = jnp.exp(sums[t : t + 1]) * carried[t : t + 1] + skip * x[t : t + 1]
        for s in range(t + 1):
            overlap = jnp.sum(write[s : s + 1] * read[t : t + 1], axis=1, keepdims=True)
            term = pushed[s : s + 1] * overlap
            if s < t:
                term = term * jnp.exp(sums[t : t + 1] - sums[s : s + 1])
            row = row + term
        readout.append(row)
    gated = jnp.concatenate(readout, axis=0) * gate
    tall = jnp.concatenate([gated[:, h * head_width : (h + 1) * head_width] for h in range(heads)], axis=0)
    tall = tall * lax.rsqrt(jnp.mean(tall * tall, axis=1, keepdims=True) + epsilon)
    m_at = q_heads * hs
    for h in range(heads):
        a = h * head_width
        own[:, m_at + a : m_at + a + head_width] = (
            tall[h * t_count : (h + 1) * t_count] * gain_ref[:, a : a + head_width]
        )
    targets, _, piece = out_ref.shape
    for i in range(targets):
        out_ref[i] = own[:, i * piece : (i + 1) * piece].astype(BF16)


def gate_up_body(xg_ref, inv_ref, gate_ref, up_ref, own_ref, send_ref):
    rows, columns = xg_ref.shape[0], gate_ref.shape[1]
    xg = xg_ref[...]
    inv = inv_ref[:, :1]
    half = own_ref.shape[1] // 2
    for w_ref, at in ((gate_ref, 0), (up_ref, half)):
        part = dot_nn(xg, w_ref[...]) * inv
        own_ref[:, at : at + columns] = part
        send_ref[:, at : at + columns] = part.astype(BF16)


def down_body(own_ref, recv_ref, down_ref, after_ref, out_ref):
    columns = down_ref.shape[0]
    half = own_ref.shape[1] // 2
    gate = own_ref[:, :columns] + recv_ref[:, :columns].astype(F32)
    up = own_ref[:, half : half + columns] + recv_ref[:, half : half + columns].astype(F32)
    hidden = (silu(gate) * up).astype(BF16)
    out_ref[...] = dot_nn(hidden, down_ref[...])


def output_body(place, mine_ref, other_ref, w_ref, ff_ref, out_ref):
    me = place[1]
    blocks, rows, piece = mine_ref.shape
    a = mine_ref[...].astype(F32).reshape(blocks * rows, piece).astype(BF16)
    b = other_ref[...].astype(F32).reshape(blocks * rows, piece).astype(BF16)
    total = ff_ref[...] + dot_nn(a, w_ref[me]) + dot_nn(b, w_ref[1 - me])
    out_ref[...] = total.reshape(blocks, rows, total.shape[1]).astype(BF16)


def on_device(
    tokens,
    norm_gain,
    mixer_in,
    shared_in,
    step_in,
    step_bias,
    decay_rate,
    skip_gain,
    cached_keys,
    cached_values,
    lengths,
    state_cache,
    mixer_gain,
    mixer_out,
    gate_weight,
    up_weight,
    down_weight,
):
    n_short = lax.axis_size("short")
    n_wide = lax.axis_size("wide")
    own_rows, width = tokens.shape
    rows = own_rows * n_wide
    columns = mixer_in.shape[2]
    shared = shared_in.shape[1]
    heads = step_bias.shape[0]
    head_width = state_cache.shape[2]
    states = state_cache.shape[3]
    q_heads = QUERY_HEADS // n_short
    kv_heads = KEY_VALUE_HEADS // n_short
    slots = cached_keys.shape[1]
    ff = gate_weight.shape[1]
    piece = mixer_out.shape[1]
    place = jnp.stack([lax.axis_index("wide"), lax.axis_index("short")]).astype(jnp.int32)
    other_core = [(0, 1), (1, 0)]

    gathered = tokens[None]
    order = [0]
    stride = n_wide // 2
    while stride:
        moved = lax.ppermute(gathered, "wide", [(j, j ^ stride) for j in range(n_wide)])
        gathered = jnp.concatenate([gathered, moved], axis=0)
        order = order + [rel ^ stride for rel in order]
        stride //= 2

    used = round_up(columns, LANES) + round_up(shared, LANES)
    sent = used + 2 * LANES
    wm = jnp.transpose(mixer_in, (1, 2, 0))
    ws = jnp.transpose(shared_in)
    wt = jnp.transpose(step_in).reshape(n_short, heads, width)
    weights = (wm.size + ws.size + wt.size) * 2
    xg, keep, send = call(
        functools.partial(project_body, order),
        (
            jax.ShapeDtypeStruct((rows, width), BF16),
            jax.ShapeDtypeStruct((rows, sent), F32),
            jax.ShapeDtypeStruct((rows, sent), F32),
        ),
        (place, gathered, norm_gain.reshape(1, width), wm, ws, wt),
        [IN_SMEM] + [IN_VMEM] * 5,
        [pltpu.VMEM((n_wide, own_rows, width), F32)],
        flops=rows * weights,
        nbytes=weights,
        name="project",
    )
    received = lax.ppermute(send, "short", other_core)
    features, inv, step_raw = call(
        functools.partial(combine_body, width * n_short, heads),
        (
            jax.ShapeDtypeStruct((n_wide, own_rows, used), BF16),
            jax.ShapeDtypeStruct((rows, LANES), F32),
            jax.ShapeDtypeStruct((own_rows, LANES), F32),
        ),
        (place, keep, received),
        [IN_SMEM, IN_VMEM, IN_VMEM],
        [pltpu.VMEM((n_wide, own_rows, LANES), F32)],
        flops=4 * rows * sent,
        nbytes=8 * rows * sent,
        name="combine",
    )
    features = lax.all_to_all(features, "wide", split_axis=0, concat_axis=0, tiled=True)

    half = round_up(ff, LANES)
    ff_own, ff_send = call(
        gate_up_body,
        (
            jax.ShapeDtypeStruct((rows, 2 * half), F32),
            jax.ShapeDtypeStruct((rows, 2 * half), BF16),
        ),
        (xg, inv, gate_weight, up_weight),
        [IN_VMEM] * 4,
        flops=4 * rows * width * ff,
        nbytes=4 * width * ff,
        name="gate_up",
    )
    ff_received = lax.ppermute(ff_send, "short", other_core)

    half_head = HEAD_SIZE // 2
    frequency = 10000.0 ** (-(jnp.arange(half_head, dtype=F32) * 2.0 / HEAD_SIZE))
    positions = lengths[0] + jnp.arange(own_rows, dtype=jnp.int32)
    angles = positions.astype(F32)[:, None] * frequency
    cos = jnp.cos(angles)
    sin = jnp.sin(angles)
    cos = jnp.concatenate([cos, cos], axis=1)
    sin = jnp.concatenate([-sin, sin], axis=1)
    mixed_rows = call(
        functools.partial(
            mixer_body,
            (columns, shared, round_up(columns, LANES), q_heads, kv_heads, heads, head_width),
        ),
        jax.ShapeDtypeStruct((n_wide, own_rows, piece), BF16),
        (
            lengths,
            features,
            step_raw,
            cos,
            sin,
            step_bias.reshape(1, heads),
            decay_rate.reshape(1, heads),
            skip_gain.reshape(1, heads),
            mixer_gain.reshape(1, heads * head_width),
            cached_keys[0],
            cached_values[0],
            state_cache.reshape(heads * head_width, states),
        ),
        [IN_SMEM] + [IN_VMEM] * 11,
        [
            pltpu.VMEM((own_rows, n_wide * columns), F32),
            pltpu.VMEM((own_rows, n_wide * shared), F32),
            pltpu.VMEM((own_rows, n_wide * piece), F32),
        ],
        flops=4 * own_rows * state_cache.size,
        nbytes=6 * state_cache.size,
        name="mixers",
    )
    returned = lax.all_to_all(mixed_rows, "wide", split_axis=0, concat_axis=0, tiled=True)
    other = lax.ppermute(returned, "short", other_core)
    ff_out = call(
        down_body,
        jax.ShapeDtypeStruct((rows, width), F32),
        (ff_own, ff_received, down_weight, mixed_rows),
        [IN_VMEM] * 3 + [ANYWHERE],
        flops=2 * rows * width * ff,
        nbytes=2 * width * ff,
        name="down",
    )
    summed = call(
        output_body,
        jax.ShapeDtypeStruct((n_wide, own_rows, width), BF16),
        (place, returned, other, mixer_out, ff_out),
        [IN_SMEM] + [IN_VMEM] * 4,
        flops=4 * rows * width * piece,
        nbytes=4 * width * piece,
        name="output",
    )
    pieces = lax.all_to_all(summed, "wide", split_axis=0, concat_axis=0, tiled=True)
    total = tokens.astype(F32) + jnp.sum(pieces.astype(F32), axis=0)
    return total.astype(BF16)


def solution(mesh):
    in_specs = (
        P(("groups", "wide"), "short"),
        P("short"),
        P("short", None, "wide"),
        P("short", "wide"),
        P("short", None),
        P("short"),
        P("short"),
        P("short"),
        P(("groups", "wide"), None, "short"),
        P(("groups", "wide"), None, "short"),
        P(("groups", "wide")),
        P(("groups", "wide"), "short", None, None),
        P("short"),
        P(None, "wide", "short"),
        P("short", "wide"),
        P("short", "wide"),
        P("wide", "short"),
    )
    out_specs = P(("groups", "wide"), "short")
    return jax.shard_map(
        on_device, mesh=mesh, in_specs=in_specs, out_specs=out_specs, check_vma=False
    )
```

```python
import functools

import jax
import jax.numpy as jnp
from jax import lax
from jax.experimental import pallas as pl
from jax.experimental.pallas import tpu as pltpu
from jax.sharding import PartitionSpec as P

QUERY_HEADS = 20
KEY_VALUE_HEADS = 4
HEAD_SIZE = 128
DRAFT_TOKENS = 4

epsilon = 1e-05
LANES = 128
BLOCK_COLUMNS = 384
BLOCK_DEPTH = 256
F32 = jnp.float32
BF16 = jnp.bfloat16

IN_VMEM = pl.BlockSpec(memory_space=pltpu.VMEM)
IN_SMEM = pl.BlockSpec(memory_space=pltpu.SMEM)
ANYWHERE = pl.BlockSpec(memory_space=pl.ANY)


def round_up(n, m):
    return -(-n // m) * m


def silu(v):
    return v / (1.0 + jnp.exp(-v))


def dot_nt(a, b):
    return lax.dot_general(a, b, (((1,), (1,)), ((), ())), preferred_element_type=F32)


def dot_nn(a, b):
    return jnp.dot(a, b, preferred_element_type=F32)


def kernel_room():
    n_wide = lax.axis_size("wide")
    return min(max(6 * n_wide // 8, 6), 48) * 2**20


def blocked_dot(x_ref, w_ref, done):
    depth, columns = w_ref.shape
    for at in range(0, columns, BLOCK_COLUMNS):
        here = slice(at, min(at + BLOCK_COLUMNS, columns))
        sums = None
        for k in range(0, depth, BLOCK_DEPTH):
            along = slice(k, min(k + BLOCK_DEPTH, depth))
            part = dot_nn(x_ref[:, along], w_ref[along, here])
            sums = part if sums is None else sums + part
        done(here, sums)


def call(body, out_shape, args, specs, scratch=(), flops=0, nbytes=0, name=None):
    outs = jax.tree.map(lambda _: IN_VMEM, out_shape)
    return pl.pallas_call(
        body,
        out_shape=out_shape,
        in_specs=specs,
        out_specs=outs,
        scratch_shapes=list(scratch),
        compiler_params=pltpu.CompilerParams(vmem_limit_bytes=kernel_room()),
        cost_estimate=pl.CostEstimate(flops=flops, bytes_accessed=nbytes, transcendentals=0),
        name=name,
    )(*args)


def tables_body(length_ref, place, gain_ref, cos_ref, sin_ref):
    rows, size = cos_ref.shape
    half = size // 2
    lane = lax.broadcasted_iota(jnp.int32, (rows, size), 1)
    row = lax.broadcasted_iota(jnp.int32, (rows, size), 0)
    index = jnp.where(lane < half, lane, lane - half).astype(F32)
    frequency = 10000.0 ** (-(index * 2.0 / size))
    angles = (length_ref[0] + row).astype(F32) * frequency
    sin = jnp.sin(angles)
    cos_ref[...] = jnp.cos(angles)
    sin_ref[...] = jnp.where(lane < half, -sin, sin)


def digits(n):
    high = n.bit_length() - 1
    out = []
    while high:
        low = max(high - 2, 0)
        out.append((low, 1 << (high - low)))
        high = low
    return out


def regroup_body(count, given, *refs):
    pieces, parts = refs[:given], refs[-count:]
    size = parts[0].shape[1]
    at = 0
    for ref in pieces:
        here = slice(at, at + ref.shape[0])
        for i, part in enumerate(parts):
            part[here] = ref[:, i * size : (i + 1) * size]
        at += ref.shape[0]


def part_shapes(n, rows, columns):
    _, count = digits(n)[0]
    return (jax.ShapeDtypeStruct((1, n // count, rows, columns), BF16),) * count


def exchange(parts, n, beside=(), other_core=False):
    levels = digits(n)
    offsets = [0]
    for level, (shift, count) in enumerate(levels):
        last = level + 1 == len(levels)
        steps = [digit << shift for digit in range(count)]
        pieces = [parts[0]] + [
            lax.ppermute(part, "wide", [(j, j ^ step) for j in range(n)])
            for step, part in zip(steps[1:], parts[1:])
        ]
        layout = [[offset ^ step for offset in offsets] for step in steps]
        offsets = sum(layout, [])
        done = list(beside[level](parts[0])) if level < len(beside) else []
        if not last:
            following = levels[level + 1][1]
            _, rest, rows, columns = pieces[0].shape
            parts = call(
                functools.partial(regroup_body, following, len(pieces)),
                (jax.ShapeDtypeStruct((len(offsets), rest // following, rows, columns), BF16),) * following,
                pieces + done,
                [IN_VMEM] * len(pieces) + [ANYWHERE] * len(done),
                name="regroup",
            )
    if not other_core:
        return pieces, layout
    other = [
        lax.ppermute(
            part, ("wide", "short"), [(2 * j + s, 2 * (j ^ step) + 1 - s) for j in range(n) for s in range(2)]
        )
        for step, part in zip(steps, parts)
    ]
    return pieces, layout, other


def place_blocks(target, at, layout, refs):
    for offsets, ref in zip(layout, refs):
        for i, offset in enumerate(offsets):
            target[at ^ offset] = ref[i, 0].astype(F32)


def join_body(*refs):
    out_ref = refs[-1]
    at = 0
    for ref in refs[:-2]:
        out_ref[at : at + ref.shape[0]] = ref[...]
        at += ref.shape[0]


def digits(n):
    high = n.bit_length() - 1
    out = []
    while high:
        low = max(high - 2, 0)
        out.append((low, 1 << (high - low)))
        high = low
    return out


def regroup_body(count, given, *refs):
    pieces, parts = refs[:given], refs[-count:]
    size = parts[0].shape[1]
    at = 0
    for ref in pieces:
        here = slice(at, at + ref.shape[0])
        for i, part in enumerate(parts):
            part[here] = ref[:, i * size : (i + 1) * size]
        at += ref.shape[0]


def part_shapes(n, rows, columns):
    _, count = digits(n)[0]
    return (jax.ShapeDtypeStruct((1, n // count, rows, columns), BF16),) * count


def exchange(parts, n, beside=(), other_core=False):
    levels = digits(n)
    offsets = [0]
    for level, (shift, count) in enumerate(levels):
        last = level + 1 == len(levels)
        steps = [digit << shift for digit in range(count)]
        pieces = [parts[0]] + [
            lax.ppermute(part, "wide", [(j, j ^ step) for j in range(n)])
            for step, part in zip(steps[1:], parts[1:])
        ]
        layout = [[offset ^ step for offset in offsets] for step in steps]
        offsets = sum(layout, [])
        done = list(beside[level](parts[0])) if level < len(beside) else []
        if not last:
            following = levels[level + 1][1]
            _, rest, rows, columns = pieces[0].shape
            parts = call(
                functools.partial(regroup_body, following, len(pieces)),
                (jax.ShapeDtypeStruct((len(offsets), rest // following, rows, columns), BF16),) * following,
                pieces + done,
                [IN_VMEM] * len(pieces) + [ANYWHERE] * len(done),
                name="regroup",
            )
    if not other_core:
        return pieces, layout
    other = [
        lax.ppermute(
            part, ("wide", "short"), [(2 * j + s, 2 * (j ^ step) + 1 - s) for j in range(n) for s in range(2)]
        )
        for step, part in zip(steps, parts)
    ]
    return pieces, layout, other


def place_blocks(target, at, layout, refs):
    for offsets, ref in zip(layout, refs):
        for i, offset in enumerate(offsets):
            target[at ^ offset] = ref[i, 0].astype(F32)


def project_body(
    shared, given, place, after, *refs
):
    x_refs, (gain_ref, wm_ref, ws_ref, wt_ref, xg_ref, send_ref, aux_ref) = refs[:given], refs[given:]
    mine = place[1]
    width = xg_ref.shape[1]
    x = jnp.concatenate(
        [ref[...].astype(F32).reshape(ref.shape[0] * ref.shape[1], width) for ref in x_refs], axis=0
    )
    squares = jnp.sum(x * x, axis=1, keepdims=True)
    xg = (x * gain_ref[...]).astype(BF16)
    xg_ref[...] = xg
    columns = wm_ref.shape[1]
    shared_at = round_up(columns, LANES)
    send_ref[:, :columns] = dot_nt(xg, wm_ref[1 - mine])
    heads = wt_ref.shape[1]
    both = dot_nt(xg, ws_ref[...])
    squares = jnp.broadcast_to(squares, (x.shape[0], LANES))
    for ref, at, group in ((send_ref, shared_at, 1 - mine), (aux_ref, 0, mine)):
        step_at = at + round_up(shared, LANES)
        ref[:, at : at + shared] = both
        ref[:, step_at : step_at + heads] = dot_nt(xg, wt_ref[group])
        ref[:, step_at + LANES :] = squares


def own_group_body(place, xg_ref, wm_ref, keep_ref):
    columns = wm_ref.shape[1]
    keep_ref[:, :columns] = dot_nt(xg_ref[...], wm_ref[place[1]])


def combine_body(width, order, keep_ref, aux_ref, recv_ref, *refs):
    parts, (inv_ref, step_ref) = refs[:-2], refs[-2:]
    rows = step_ref.shape[0]
    first = keep_ref.shape[1]
    aux = aux_ref[...] + recv_ref[:, first:]
    inv = lax.rsqrt(aux[:, -LANES:] / width + epsilon)
    inv_ref[...] = inv
    at = order.index(0) * rows
    step = aux[:, -2 * LANES : -LANES] * inv
    step_ref[...] = step[at : at + rows]
    feat = (keep_ref[...] + recv_ref[:, :first]) * inv[:, :1]
    more = aux[:, : -2 * LANES] * inv[:, :1]
    size = parts[0].shape[1]
    for i, part in enumerate(parts):
        for j in range(size):
            at = order.index(i * size + j) * rows
            part[0, j, :, :first] = feat[at : at + rows].astype(BF16)
            part[0, j, :, first:] = more[at : at + rows].astype(BF16)


def spread_blocks(wide_at, source, parts):
    size = parts[0].shape[1]
    for i, part in enumerate(parts):
        for j in range(size):
            part[0, j] = source[wide_at ^ (i * size + j)].astype(BF16)


def mixer_body(dims, layout, out_count, length_ref, place, *refs):
    feat_refs, refs = refs[: len(layout)], refs[len(layout) :]
    step_ref, cos_ref, sin_ref, bias_ref, decay_ref, skip_ref, gain_ref = refs[:7]
    key_ref, value_ref, state_ref = refs[7:10]
    parts = refs[11 : 11 + out_count]
    feat, fs, bc, own, cut = refs[11 + out_count :]
    place_blocks(feat, place[0], layout, feat_refs)
    columns, shared, shared_at, q_heads, kv_heads, heads, head_width = dims
    t_count = DRAFT_TOKENS
    hs = HEAD_SIZE
    repeat = q_heads // kv_heads
    for i in range(feat.shape[0]):
        fs[:, i * columns : (i + 1) * columns] = feat[i, :, :columns]
        bc[:, i * shared : (i + 1) * shared] = feat[i, :, shared_at : shared_at + shared]
    length = length_ref[0]

    turned = q_heads + kv_heads
    stacked = jnp.concatenate([fs[:, h * hs : (h + 1) * hs] for h in range(turned)], axis=0)
    cos = jnp.concatenate([cos_ref[...]] * turned, axis=0)
    sin = jnp.concatenate([sin_ref[...]] * turned, axis=0)
    swapped = jnp.concatenate([stacked[:, hs // 2 :], stacked[:, : hs // 2]], axis=1)
    rotated = stacked * cos + swapped * sin
    slots = key_ref.shape[0]
    scale = hs ** (-0.5)
    group_rows = repeat * t_count
    live = lax.broadcasted_iota(jnp.int32, (group_rows, slots), 1) < length
    row_t = lax.broadcasted_iota(jnp.int32, (group_rows, LANES), 0) % t_count
    causal = lax.broadcasted_iota(jnp.int32, (group_rows, LANES), 1) <= row_t
    filler = jnp.zeros((LANES - t_count, hs), F32)
    for k in range(kv_heads):
        queries = rotated[k * group_rows : (k + 1) * group_rows].astype(BF16)
        at = q_heads * t_count + k * t_count
        new_keys = jnp.concatenate([rotated[at : at + t_count], filler], axis=0).astype(BF16)
        v_at = (turned + k) * hs
        new_values = jnp.concatenate([fs[:, v_at : v_at + hs], filler], axis=0).astype(BF16)
        head = slice(k * hs, (k + 1) * hs)
        cache = jnp.where(live, dot_nt(queries, key_ref[:, head]) * scale, -1e30)
        fresh = jnp.where(causal, dot_nt(queries, new_keys) * scale, -1e30)
        highest = jnp.maximum(
            jnp.max(cache, axis=1, keepdims=True), jnp.max(fresh, axis=1, keepdims=True)
        )
        cache = jnp.exp(cache - highest)
        fresh = jnp.exp(fresh - highest)
        total = jnp.sum(cache, axis=1, keepdims=True) + jnp.sum(fresh, axis=1, keepdims=True)
        attended = dot_nn((cache / total).astype(BF16), value_ref[:, head]) + dot_nn(
            (fresh / total).astype(BF16), new_values
        )
        for r in range(repeat):
            h = k * repeat + r
            own[:, h * hs : (h + 1) * hs] = attended[r * t_count : (r + 1) * t_count]

    x_at = (turned + kv_heads) * hs
    m_size = heads * head_width
    states = bc.shape[1] // 2
    write = silu(bc[:, :states])
    read = silu(bc[:, states:])
    read_high = read.astype(BF16)
    read_low = (read - read_high.astype(F32)).astype(BF16)
    carried = dot_nt(read_high, state_ref[...]) + dot_nt(read_low, state_ref[...])
    count = heads * t_count

    def tall(v, at):
        return jnp.concatenate(
            [v[:, at + h * head_width : at + (h + 1) * head_width] for h in range(heads)], axis=0
        )

    row_head = lax.broadcasted_iota(jnp.int32, (count, heads), 0) // t_count
    mine = row_head == lax.broadcasted_iota(jnp.int32, (count, heads), 1)

    def column(v):
        if v.shape[0] > 1:
            v = jnp.concatenate([v] * heads, axis=0)
        return jnp.sum(jnp.where(mine, v, 0.0), axis=1, keepdims=True)

    wide = (count, head_width)
    token = lax.broadcasted_iota(jnp.int32, wide, 0) % t_count

    def earlier(v, d):
        moved = jnp.concatenate([v[count - d :], v[: count - d]], axis=0)
        return jnp.where(token >= d, moved, 0.0)

    raw = step_ref[:, :heads] + bias_ref[...]
    step = jnp.maximum(raw, 0.0) + jnp.log1p(jnp.exp(-jnp.abs(raw)))
    rate = jnp.broadcast_to(column(-step * decay_ref[...]), wide)
    sums = rate
    for d in range(1, t_count):
        sums = sums + earlier(rate, d)
    x = silu(tall(fs, x_at))
    gate = silu(tall(fs, x_at + m_size))
    pushed = column(step) * x
    readout = jnp.exp(sums) * tall(carried, 0) + column(skip_ref[...]) * x
    since = jnp.zeros(wide, F32)
    for d in range(t_count):
        before = write if d == 0 else jnp.concatenate([write[t_count - d :], write[: t_count - d]], axis=0)
        overlap = jnp.sum(before * read, axis=1, keepdims=True)
        overlap = jnp.concatenate([overlap] * heads, axis=0)
        if d == 0:
            readout = readout + overlap * pushed
        else:
            since = since + (rate if d == 1 else earlier(rate, d - 1))
            readout = readout + overlap * jnp.exp(since) * earlier(pushed, d)
    gated = readout * gate
    gated = gated * lax.rsqrt(jnp.mean(gated * gated, axis=1, keepdims=True) + epsilon)
    m_at = q_heads * hs
    for h in range(heads):
        at = h * head_width
        own[:, m_at + at : m_at + at + head_width] = (
            gated[h * t_count : (h + 1) * t_count] * gain_ref[:, at : at + head_width]
        )
    targets, _, piece = cut.shape
    for i in range(targets):
        cut[i] = own[:, i * piece : (i + 1) * piece]
    spread_blocks(place[0], cut, parts)


def gate_body(xg_ref, inv_ref, gate_ref, own_ref):
    def done(here, sums):
        own_ref[:, here] = sums * inv_ref[:, :1]

    blocked_dot(xg_ref, gate_ref, done)


def up_body(xg_ref, inv_ref, up_ref, gate_own_ref, after_ref, own_ref, send_ref):
    def done(here, sums):
        part = sums * inv_ref[:, :1]
        own_ref[:, here] = part
        send_ref[0, :, here] = gate_own_ref[:, here].astype(BF16)
        send_ref[1, :, here] = part.astype(BF16)

    blocked_dot(xg_ref, up_ref, done)


def down_body(gate_ref, up_ref, recv_ref, down_ref, after_ref, out_ref, hidden_ref):
    gate = gate_ref[...] + recv_ref[0].astype(F32)
    up = up_ref[...] + recv_ref[1].astype(F32)
    hidden_ref[...] = (silu(gate) * up).astype(BF16)

    def done(here, sums):
        out_ref[:, here] = sums

    blocked_dot(hidden_ref, down_ref, done)


def output_body(layout, order, place, *refs):
    count = len(layout)
    mine, other = refs[:count], refs[count : 2 * count]
    w_ref, ff_ref, out_ref = refs[2 * count :]
    wide_at, me = place[0], place[1]
    rows = out_ref.shape[1]
    senders = [offset for offsets in layout for offset in offsets]
    total = ff_ref[...]
    for part, group in ((mine, me), (other, 1 - me)):
        blocks = [ref[i, 0].astype(F32) for ref in part for i in range(ref.shape[0])]
        x = jnp.concatenate([blocks[senders.index(offset)] for offset in order], axis=0)
        total = total + dot_nn(x.astype(BF16), w_ref[group])
    for i, offset in enumerate(order):
        out_ref[wide_at ^ offset] = total[i * rows : (i + 1) * rows].astype(BF16)


def on_device(
    tokens,
    norm_gain,
    mixer_in,
    shared_in,
    step_in,
    step_bias,
    decay_rate,
    skip_gain,
    cached_keys,
    cached_values,
    lengths,
    state_cache,
    mixer_gain,
    mixer_out,
    gate_weight,
    up_weight,
    down_weight,
):
    n_short = lax.axis_size("short")
    n_wide = lax.axis_size("wide")
    own_rows, width = tokens.shape
    rows = own_rows * n_wide
    columns = mixer_in.shape[2]
    shared = shared_in.shape[1]
    heads = step_bias.shape[0]
    head_width = state_cache.shape[2]
    states = state_cache.shape[3]
    q_heads = QUERY_HEADS // n_short
    kv_heads = KEY_VALUE_HEADS // n_short
    slots = cached_keys.shape[1]
    ff = gate_weight.shape[1]
    piece = mixer_out.shape[1]
    place = jnp.stack([lax.axis_index("wide"), lax.axis_index("short")]).astype(jnp.int32)
    other_core = [(0, 1), (1, 0)]
    gain = norm_gain.reshape(1, width)

    cos, sin = call(
        tables_body,
        (jax.ShapeDtypeStruct((own_rows, HEAD_SIZE), F32), jax.ShapeDtypeStruct((own_rows, HEAD_SIZE), F32)),
        (lengths, place, gain),
        [IN_SMEM, IN_SMEM, ANYWHERE],
        flops=10**11,
        nbytes=10**8,
        name="tables",
    )

    held = tokens[None]
    offsets = [0]
    for shift, count in digits(n_wide):
        steps = [digit << shift for digit in range(1, count)]
        pieces = [held] + [
            lax.ppermute(held, "wide", [(j, j ^ step) for j in range(n_wide)]) for step in steps
        ]
        offsets = [[rel ^ step for rel in offsets] for step in [0] + steps]
        layout, offsets = offsets, sum(offsets, [])
        if shift:
            held = call(
                join_body,
                jax.ShapeDtypeStruct((len(offsets), own_rows, width), BF16),
                pieces + [cos],
                [IN_VMEM] * len(pieces) + [ANYWHERE],
                name="join",
            )
    used = round_up(columns, LANES) + round_up(shared, LANES)
    sent = used + 2 * LANES
    wm = jnp.transpose(mixer_in, (1, 2, 0))
    ws = jnp.transpose(shared_in)
    wt = jnp.transpose(step_in).reshape(n_short, heads, width)
    weights = (wm.size + ws.size + wt.size) * 2
    order = sum(layout, [])
    xg, send, aux = call(
        functools.partial(project_body, shared, len(pieces)),
        (
            jax.ShapeDtypeStruct((rows, width), BF16),
            jax.ShapeDtypeStruct((rows, sent), F32),
            jax.ShapeDtypeStruct((rows, sent - round_up(columns, LANES)), F32),
        ),
        (place, cos, *pieces, gain, wm, ws, wt),
        [IN_SMEM, ANYWHERE] + [IN_VMEM] * (len(pieces) + 4),
        flops=rows * weights,
        nbytes=20 * weights,
        name="project",
    )
    received = lax.ppermute(send, "short", other_core)
    keep = call(
        own_group_body,
        jax.ShapeDtypeStruct((rows, round_up(columns, LANES)), F32),
        (place, xg, wm),
        [IN_SMEM, IN_VMEM, IN_VMEM],
        flops=rows * weights,
        nbytes=weights // 2,
        name="own_group",
    )
    *parts, inv, step_raw = call(
        functools.partial(combine_body, width * n_short, order),
        part_shapes(n_wide, own_rows, used)
        + (
            jax.ShapeDtypeStruct((rows, LANES), F32),
            jax.ShapeDtypeStruct((own_rows, LANES), F32),
        ),
        (keep, aux, received),
        [IN_VMEM] * 3,
        flops=4 * rows * sent,
        nbytes=8 * rows * sent,
        name="combine",
    )
    made = []

    def gate(after):
        made.append(
            call(
                gate_body,
                jax.ShapeDtypeStruct((rows, ff), F32),
                (xg, inv, gate_weight),
                [IN_VMEM] * 3,
                flops=2 * rows * width * ff,
                nbytes=2 * width * ff,
                name="gate",
            )
        )
        return made

    def up(after):
        made.extend(
            call(
                up_body,
                (jax.ShapeDtypeStruct((rows, ff), F32), jax.ShapeDtypeStruct((2, rows, ff), BF16)),
                (xg, inv, up_weight, made[0], after),
                [IN_VMEM] * 4 + [ANYWHERE],
                flops=2 * rows * width * ff,
                nbytes=2 * width * ff,
                name="up",
            )
        )
        return made[1:]

    features, layout = exchange(parts, n_wide, (gate, up))
    gate_own, up_own, ff_send = made
    features, ff_send = lax.optimization_barrier((features, ff_send))
    ff_received = lax.ppermute(ff_send, "short", other_core)
    out_shapes = part_shapes(n_wide, own_rows, piece)
    parts = call(
        functools.partial(
            mixer_body,
            (columns, shared, round_up(columns, LANES), q_heads, kv_heads, heads, head_width),
            layout,
            len(out_shapes),
        ),
        out_shapes,
        (
            lengths,
            place,
            *features,
            step_raw,
            cos,
            sin,
            step_bias.reshape(1, heads),
            decay_rate.reshape(1, heads),
            skip_gain.reshape(1, heads),
            mixer_gain.reshape(1, heads * head_width),
            cached_keys[0],
            cached_values[0],
            state_cache.reshape(heads * head_width, states),
            up_own,
        ),
        [IN_SMEM] * 2 + [IN_VMEM] * (len(features) + 10) + [ANYWHERE],
        [
            pltpu.VMEM((n_wide, own_rows, used), F32),
            pltpu.VMEM((own_rows, n_wide * columns), F32),
            pltpu.VMEM((own_rows, n_wide * shared), F32),
            pltpu.VMEM((own_rows, n_wide * piece), F32),
            pltpu.VMEM((n_wide, own_rows, piece), F32),
        ],
        flops=4 * own_rows * state_cache.size,
        nbytes=6 * state_cache.size,
        name="mixers",
    )
    ff_out = []

    def down(after):
        ff_out.append(
            call(
                down_body,
                jax.ShapeDtypeStruct((rows, width), F32),
                (gate_own, up_own, ff_received, down_weight, after),
                [IN_VMEM] * 4 + [ANYWHERE],
                [pltpu.VMEM((rows, ff), BF16)],
                flops=2 * rows * width * ff,
                nbytes=2 * width * ff,
                name="down",
            )
        )
        return ff_out

    mine, layout, other = exchange(parts, n_wide, (down,), other_core=True)
    summed = call(
        functools.partial(output_body, layout, order),
        jax.ShapeDtypeStruct((n_wide, own_rows, width), BF16),
        (place, *mine, *other, mixer_out, ff_out[0]),
        [IN_SMEM] + [IN_VMEM] * (2 * len(mine) + 2),
        flops=4 * rows * width * piece,
        nbytes=4 * width * piece,
        name="output",
    )
    pieces = lax.all_to_all(summed, "wide", split_axis=0, concat_axis=0, tiled=True)
    total = tokens.astype(F32) + jnp.sum(pieces.astype(F32), axis=0)
    return total.astype(BF16)


def solution(mesh):
    in_specs = (
        P(("groups", "wide"), "short"),
        P("short"),
        P("short", None, "wide"),
        P("short", "wide"),
        P("short", None),
        P("short"),
        P("short"),
        P("short"),
        P(("groups", "wide"), None, "short"),
        P(("groups", "wide"), None, "short"),
        P(("groups", "wide")),
        P(("groups", "wide"), "short", None, None),
        P("short"),
        P(None, "wide", "short"),
        P("short", "wide"),
        P("short", "wide"),
        P("wide", "short"),
    )
    out_specs = P(("groups", "wide"), "short")
    return jax.shard_map(
        on_device, mesh=mesh, in_specs=in_specs, out_specs=out_specs, check_vma=False
    )
```

```python
import functools

import jax
import jax.numpy as jnp
from jax import lax
from jax.experimental import pallas as pl
from jax.experimental.pallas import tpu as pltpu
from jax.sharding import PartitionSpec as P

QUERY_HEADS = 20
KEY_VALUE_HEADS = 4
HEAD_SIZE = 128
DRAFT_TOKENS = 4

epsilon = 1e-05
LANES = 128
BLOCK_COLUMNS = 384
BLOCK_DEPTH = 256
F32 = jnp.float32
BF16 = jnp.bfloat16

IN_VMEM = pl.BlockSpec(memory_space=pltpu.VMEM)
IN_SMEM = pl.BlockSpec(memory_space=pltpu.SMEM)
ANYWHERE = pl.BlockSpec(memory_space=pl.ANY)


def round_up(n, m):
    return -(-n // m) * m


def silu(v):
    return v / (1.0 + jnp.exp(-v))


def dot_nt(a, b):
    return lax.dot_general(a, b, (((1,), (1,)), ((), ())), preferred_element_type=F32)


def dot_nn(a, b):
    return jnp.dot(a, b, preferred_element_type=F32)


def kernel_room():
    n_wide = lax.axis_size("wide")
    return min(max(6 * n_wide // 8, 6), 48) * 2**20


def blocked_dot(x_ref, w_ref, done):
    depth, columns = w_ref.shape
    for at in range(0, columns, BLOCK_COLUMNS):
        here = slice(at, min(at + BLOCK_COLUMNS, columns))
        sums = None
        for k in range(0, depth, BLOCK_DEPTH):
            along = slice(k, min(k + BLOCK_DEPTH, depth))
            part = dot_nn(x_ref[:, along], w_ref[along, here])
            sums = part if sums is None else sums + part
        done(here, sums)


def call(body, out_shape, args, specs, scratch=(), flops=0, nbytes=0, name=None):
    outs = jax.tree.map(lambda _: IN_VMEM, out_shape)
    return pl.pallas_call(
        body,
        out_shape=out_shape,
        in_specs=specs,
        out_specs=outs,
        scratch_shapes=list(scratch),
        compiler_params=pltpu.CompilerParams(vmem_limit_bytes=kernel_room()),
        cost_estimate=pl.CostEstimate(flops=flops, bytes_accessed=nbytes, transcendentals=0),
        name=name,
    )(*args)


def tables_body(length_ref, place, gain_ref, cos_ref, sin_ref):
    rows, size = cos_ref.shape
    half = size // 2
    lane = lax.broadcasted_iota(jnp.int32, (rows, size), 1)
    row = lax.broadcasted_iota(jnp.int32, (rows, size), 0)
    index = jnp.where(lane < half, lane, lane - half).astype(F32)
    frequency = 10000.0 ** (-(index * 2.0 / size))
    angles = (length_ref[0] + row).astype(F32) * frequency
    sin = jnp.sin(angles)
    cos_ref[...] = jnp.cos(angles)
    sin_ref[...] = jnp.where(lane < half, -sin, sin)


def digits(n, first=2):
    high = n.bit_length() - 1
    out = []
    while high:
        low = max(high - (2 if out else first), 0)
        out.append((low, 1 << (high - low)))
        high = low
    return out


def regroup_body(count, given, *refs):
    pieces, parts = refs[:given], refs[-count:]
    size = parts[0].shape[1]
    at = 0
    for ref in pieces:
        here = slice(at, at + ref.shape[0])
        for i, part in enumerate(parts):
            part[here] = ref[:, i * size : (i + 1) * size]
        at += ref.shape[0]


def part_shapes(n, rows, columns, first=2):
    _, count = digits(n, first)[0]
    return (jax.ShapeDtypeStruct((1, n // count, rows, columns), BF16),) * count


def exchange(parts, n, beside=(), other_core=False, first=2):
    levels = digits(n, first)
    offsets = [0]
    for level, (shift, count) in enumerate(levels):
        last = level + 1 == len(levels)
        steps = [digit << shift for digit in range(count)]
        pieces = [parts[0]] + [
            lax.ppermute(part, "wide", [(j, j ^ step) for j in range(n)])
            for step, part in zip(steps[1:], parts[1:])
        ]
        layout = [[offset ^ step for offset in offsets] for step in steps]
        offsets = sum(layout, [])
        done = list(beside[level](parts[0])) if level < len(beside) else []
        if not last:
            following = levels[level + 1][1]
            _, rest, rows, columns = pieces[0].shape
            parts = call(
                functools.partial(regroup_body, following, len(pieces)),
                (jax.ShapeDtypeStruct((len(offsets), rest // following, rows, columns), BF16),) * following,
                pieces + done,
                [IN_VMEM] * len(pieces) + [ANYWHERE] * len(done),
                name="regroup",
            )
    if not other_core:
        return pieces, layout
    other = [
        lax.ppermute(
            part, ("wide", "short"), [(2 * j + s, 2 * (j ^ step) + 1 - s) for j in range(n) for s in range(2)]
        )
        for step, part in zip(steps, parts)
    ]
    return pieces, layout, other


def place_blocks(target, at, layout, refs):
    for offsets, ref in zip(layout, refs):
        for i, offset in enumerate(offsets):
            target[at ^ offset, : ref.shape[2]] = ref[i, 0].astype(F32)


def join_body(*refs):
    out_ref = refs[-1]
    at = 0
    for ref in refs[:-2]:
        out_ref[at : at + ref.shape[0]] = ref[...]
        at += ref.shape[0]


def digits(n, first=2):
    high = n.bit_length() - 1
    out = []
    while high:
        low = max(high - (2 if out else first), 0)
        out.append((low, 1 << (high - low)))
        high = low
    return out


def regroup_body(count, given, *refs):
    pieces, parts = refs[:given], refs[-count:]
    size = parts[0].shape[1]
    at = 0
    for ref in pieces:
        here = slice(at, at + ref.shape[0])
        for i, part in enumerate(parts):
            part[here] = ref[:, i * size : (i + 1) * size]
        at += ref.shape[0]


def part_shapes(n, rows, columns, first=2):
    _, count = digits(n, first)[0]
    return (jax.ShapeDtypeStruct((1, n // count, rows, columns), BF16),) * count


def exchange(parts, n, beside=(), other_core=False, first=2):
    levels = digits(n, first)
    offsets = [0]
    for level, (shift, count) in enumerate(levels):
        last = level + 1 == len(levels)
        steps = [digit << shift for digit in range(count)]
        pieces = [parts[0]] + [
            lax.ppermute(part, "wide", [(j, j ^ step) for j in range(n)])
            for step, part in zip(steps[1:], parts[1:])
        ]
        layout = [[offset ^ step for offset in offsets] for step in steps]
        offsets = sum(layout, [])
        done = list(beside[level](parts[0])) if level < len(beside) else []
        if not last:
            following = levels[level + 1][1]
            _, rest, rows, columns = pieces[0].shape
            parts = call(
                functools.partial(regroup_body, following, len(pieces)),
                (jax.ShapeDtypeStruct((len(offsets), rest // following, rows, columns), BF16),) * following,
                pieces + done,
                [IN_VMEM] * len(pieces) + [ANYWHERE] * len(done),
                name="regroup",
            )
    if not other_core:
        return pieces, layout
    other = [
        lax.ppermute(
            part, ("wide", "short"), [(2 * j + s, 2 * (j ^ step) + 1 - s) for j in range(n) for s in range(2)]
        )
        for step, part in zip(steps, parts)
    ]
    return pieces, layout, other


def place_blocks(target, at, layout, refs):
    for offsets, ref in zip(layout, refs):
        for i, offset in enumerate(offsets):
            target[at ^ offset, : ref.shape[2]] = ref[i, 0].astype(F32)


def project_body(
    shared, given, place, after, *refs
):
    x_refs, (gain_ref, wm_ref, ws_ref, wt_ref, xg_ref, send_ref, aux_ref) = refs[:given], refs[given:]
    mine = place[1]
    width = xg_ref.shape[1]
    x = jnp.concatenate(
        [ref[...].astype(F32).reshape(ref.shape[0] * ref.shape[1], width) for ref in x_refs], axis=0
    )
    squares = jnp.sum(x * x, axis=1, keepdims=True)
    xg = (x * gain_ref[...]).astype(BF16)
    xg_ref[...] = xg
    columns = wm_ref.shape[1]
    shared_at = round_up(columns, LANES)
    send_ref[:, :columns] = dot_nt(xg, wm_ref[1 - mine])
    heads = wt_ref.shape[1]
    both = dot_nt(xg, ws_ref[...])
    squares = jnp.broadcast_to(squares, (x.shape[0], LANES))
    for ref, at, group in ((send_ref, shared_at, 1 - mine), (aux_ref, 0, mine)):
        step_at = at + round_up(shared, LANES)
        ref[:, at : at + shared] = both
        ref[:, step_at : step_at + heads] = dot_nt(xg, wt_ref[group])
        ref[:, step_at + LANES :] = squares


def own_group_body(place, xg_ref, wm_ref, keep_ref):
    columns = wm_ref.shape[1]
    keep_ref[:, :columns] = dot_nt(xg_ref[...], wm_ref[place[1]])


def combine_body(width, order, keep_ref, aux_ref, recv_ref, *refs):
    parts, (inv_ref, step_ref) = refs[:-2], refs[-2:]
    rows = step_ref.shape[0]
    first = keep_ref.shape[1]
    aux = aux_ref[...] + recv_ref[:, first:]
    inv = lax.rsqrt(aux[:, -LANES:] / width + epsilon)
    inv_ref[...] = inv
    at = order.index(0) * rows
    step = aux[:, -2 * LANES : -LANES] * inv
    step_ref[...] = step[at : at + rows]
    feat = (keep_ref[...] + recv_ref[:, :first]) * inv[:, :1]
    more = aux[:, : -2 * LANES] * inv[:, :1]
    size = parts[0].shape[1]
    for i, part in enumerate(parts):
        for j in range(size):
            at = order.index(i * size + j) * rows
            part[0, j, :, :first] = feat[at : at + rows].astype(BF16)
            part[0, j, :, first:] = more[at : at + rows].astype(BF16)


def spread_blocks(wide_at, source, parts):
    size = parts[0].shape[1]
    for i, part in enumerate(parts):
        for j in range(size):
            part[0, j] = source[wide_at ^ (i * size + j), : part.shape[2]].astype(BF16)


def mixer_body(dims, layout, out_count, length_ref, place, *refs):
    feat_refs, refs = refs[: len(layout)], refs[len(layout) :]
    step_ref, cos_ref, sin_ref, bias_ref, decay_ref, skip_ref, gain_ref = refs[:7]
    key_ref, value_ref, state_ref = refs[7:10]
    parts = refs[11 : 11 + out_count]
    feat, fs, bc, own, cut = refs[11 + out_count :]
    place_blocks(feat, place[0], layout, feat_refs)
    columns, shared, shared_at, q_heads, kv_heads, heads, head_width = dims
    t_count = DRAFT_TOKENS
    hs = HEAD_SIZE
    repeat = q_heads // kv_heads
    for i in range(feat.shape[0]):
        fs[:t_count, i * columns : (i + 1) * columns] = feat[i, :t_count, :columns]
        bc[:t_count, i * shared : (i + 1) * shared] = feat[i, :t_count, shared_at : shared_at + shared]
    length = length_ref[0]

    turned = q_heads + kv_heads
    stacked = jnp.concatenate([fs[:t_count, h * hs : (h + 1) * hs] for h in range(turned)], axis=0)
    cos = jnp.concatenate([cos_ref[...]] * turned, axis=0)
    sin = jnp.concatenate([sin_ref[...]] * turned, axis=0)
    swapped = jnp.concatenate([stacked[:, hs // 2 :], stacked[:, : hs // 2]], axis=1)
    rotated = stacked * cos + swapped * sin
    slots = key_ref.shape[0]
    scale = hs ** (-0.5)
    group_rows = repeat * t_count
    live = lax.broadcasted_iota(jnp.int32, (group_rows, slots), 1) < length
    row_t = lax.broadcasted_iota(jnp.int32, (group_rows, LANES), 0) % t_count
    causal = lax.broadcasted_iota(jnp.int32, (group_rows, LANES), 1) <= row_t
    filler = jnp.zeros((LANES - t_count, hs), F32)
    for k in range(kv_heads):
        queries = rotated[k * group_rows : (k + 1) * group_rows].astype(BF16)
        at = q_heads * t_count + k * t_count
        new_keys = jnp.concatenate([rotated[at : at + t_count], filler], axis=0).astype(BF16)
        v_at = (turned + k) * hs
        new_values = jnp.concatenate([fs[:t_count, v_at : v_at + hs], filler], axis=0).astype(BF16)
        head = slice(k * hs, (k + 1) * hs)
        cache = jnp.where(live, dot_nt(queries, key_ref[:, head]) * scale, -1e30)
        fresh = jnp.where(causal, dot_nt(queries, new_keys) * scale, -1e30)
        highest = jnp.maximum(
            jnp.max(cache, axis=1, keepdims=True), jnp.max(fresh, axis=1, keepdims=True)
        )
        cache = jnp.exp(cache - highest)
        fresh = jnp.exp(fresh - highest)
        total = jnp.sum(cache, axis=1, keepdims=True) + jnp.sum(fresh, axis=1, keepdims=True)
        attended = dot_nn((cache / total).astype(BF16), value_ref[:, head]) + dot_nn(
            (fresh / total).astype(BF16), new_values
        )
        for r in range(repeat):
            h = k * repeat + r
            own[:t_count, h * hs : (h + 1) * hs] = attended[r * t_count : (r + 1) * t_count]

    x_at = (turned + kv_heads) * hs
    m_size = heads * head_width
    states = bc.shape[1] // 2
    write = silu(bc[:t_count, :states])
    read = silu(bc[:t_count, states:])
    read_high = read.astype(BF16)
    read_low = (read - read_high.astype(F32)).astype(BF16)
    both = jnp.concatenate([read_high.astype(F32), read_low.astype(F32)], axis=0).astype(BF16)
    both = dot_nt(both, state_ref[...])
    carried = both[:t_count] + both[t_count:]
    count = heads * t_count

    def tall(v, at):
        return jnp.concatenate(
            [v[:t_count, at + h * head_width : at + (h + 1) * head_width] for h in range(heads)], axis=0
        )

    row_head = lax.broadcasted_iota(jnp.int32, (count, heads), 0) // t_count
    mine = row_head == lax.broadcasted_iota(jnp.int32, (count, heads), 1)

    def column(v):
        if v.shape[0] > 1:
            v = jnp.concatenate([v] * heads, axis=0)
        return jnp.sum(jnp.where(mine, v, 0.0), axis=1, keepdims=True)

    wide = (count, head_width)
    token = lax.broadcasted_iota(jnp.int32, wide, 0) % t_count

    def earlier(v, d):
        moved = jnp.concatenate([v[count - d :], v[: count - d]], axis=0)
        return jnp.where(token >= d, moved, 0.0)

    raw = step_ref[:, :heads] + bias_ref[...]
    step = jnp.maximum(raw, 0.0) + jnp.log1p(jnp.exp(-jnp.abs(raw)))
    rate = jnp.broadcast_to(column(-step * decay_ref[...]), wide)
    sums = rate
    for d in range(1, t_count):
        sums = sums + earlier(rate, d)
    x = silu(tall(fs, x_at))
    gate = silu(tall(fs, x_at + m_size))
    pushed = column(step) * x
    readout = jnp.exp(sums) * tall(carried, 0) + column(skip_ref[...]) * x
    since = jnp.zeros(wide, F32)
    for d in range(t_count):
        before = write if d == 0 else jnp.concatenate([write[t_count - d :], write[: t_count - d]], axis=0)
        overlap = jnp.sum(before * read, axis=1, keepdims=True)
        overlap = jnp.concatenate([overlap] * heads, axis=0)
        if d == 0:
            readout = readout + overlap * pushed
        else:
            since = since + (rate if d == 1 else earlier(rate, d - 1))
            readout = readout + overlap * jnp.exp(since) * earlier(pushed, d)
    gated = readout * gate
    gated = gated * lax.rsqrt(jnp.mean(gated * gated, axis=1, keepdims=True) + epsilon)
    m_at = q_heads * hs
    for h in range(heads):
        at = h * head_width
        own[:t_count, m_at + at : m_at + at + head_width] = (
            gated[h * t_count : (h + 1) * t_count] * gain_ref[:, at : at + head_width]
        )
    targets, _, piece = cut.shape
    for i in range(targets):
        cut[i, :t_count] = own[:t_count, i * piece : (i + 1) * piece]
    spread_blocks(place[0], cut, parts)


def gate_body(xg_ref, inv_ref, gate_ref, own_ref):
    def done(here, sums):
        own_ref[:, here] = sums * inv_ref[:, :1]

    blocked_dot(xg_ref, gate_ref, done)


def up_body(xg_ref, inv_ref, up_ref, gate_own_ref, after_ref, own_ref, send_ref):
    def done(here, sums):
        part = sums * inv_ref[:, :1]
        own_ref[:, here] = part
        send_ref[0, :, here] = gate_own_ref[:, here].astype(BF16)
        send_ref[1, :, here] = part.astype(BF16)

    blocked_dot(xg_ref, up_ref, done)


def down_body(gate_ref, up_ref, recv_ref, down_ref, after_ref, out_ref, hidden_ref):
    gate = gate_ref[...] + recv_ref[0].astype(F32)
    up = up_ref[...] + recv_ref[1].astype(F32)
    hidden_ref[...] = (silu(gate) * up).astype(BF16)

    def done(here, sums):
        out_ref[:, here] = sums

    blocked_dot(hidden_ref, down_ref, done)


def output_body(layout, order, place, *refs):
    count = len(layout)
    mine, other = refs[:count], refs[count : 2 * count]
    w_ref, ff_ref, out_ref = refs[2 * count :]
    wide_at, me = place[0], place[1]
    rows = out_ref.shape[1]
    senders = [offset for offsets in layout for offset in offsets]
    total = ff_ref[...]
    for part, group in ((mine, me), (other, 1 - me)):
        blocks = [ref[i, 0].astype(F32) for ref in part for i in range(ref.shape[0])]
        x = jnp.concatenate([blocks[senders.index(offset)] for offset in order], axis=0)
        total = total + dot_nn(x.astype(BF16), w_ref[group])
    for i, offset in enumerate(order):
        out_ref[wide_at ^ offset] = total[i * rows : (i + 1) * rows].astype(BF16)


def on_device(
    tokens,
    norm_gain,
    mixer_in,
    shared_in,
    step_in,
    step_bias,
    decay_rate,
    skip_gain,
    cached_keys,
    cached_values,
    lengths,
    state_cache,
    mixer_gain,
    mixer_out,
    gate_weight,
    up_weight,
    down_weight,
):
    n_short = lax.axis_size("short")
    n_wide = lax.axis_size("wide")
    own_rows, width = tokens.shape
    rows = own_rows * n_wide
    columns = mixer_in.shape[2]
    shared = shared_in.shape[1]
    heads = step_bias.shape[0]
    head_width = state_cache.shape[2]
    states = state_cache.shape[3]
    q_heads = QUERY_HEADS // n_short
    kv_heads = KEY_VALUE_HEADS // n_short
    slots = cached_keys.shape[1]
    ff = gate_weight.shape[1]
    piece = mixer_out.shape[1]
    place = jnp.stack([lax.axis_index("wide"), lax.axis_index("short")]).astype(jnp.int32)
    other_core = [(0, 1), (1, 0)]
    gain = norm_gain.reshape(1, width)

    cos, sin = call(
        tables_body,
        (jax.ShapeDtypeStruct((own_rows, HEAD_SIZE), F32), jax.ShapeDtypeStruct((own_rows, HEAD_SIZE), F32)),
        (lengths, place, gain),
        [IN_SMEM, IN_SMEM, ANYWHERE],
        flops=10**11,
        nbytes=10**8,
        name="tables",
    )

    held = tokens[None]
    offsets = [0]
    for shift, count in digits(n_wide, 1):
        steps = [digit << shift for digit in range(1, count)]
        pieces = [held] + [
            lax.ppermute(held, "wide", [(j, j ^ step) for j in range(n_wide)]) for step in steps
        ]
        offsets = [[rel ^ step for rel in offsets] for step in [0] + steps]
        layout, offsets = offsets, sum(offsets, [])
        if shift:
            held = call(
                join_body,
                jax.ShapeDtypeStruct((len(offsets), own_rows, width), BF16),
                pieces + [cos],
                [IN_VMEM] * len(pieces) + [ANYWHERE],
                name="join",
            )
    used = round_up(columns, LANES) + round_up(shared, LANES)
    sent = used + 2 * LANES
    wm = jnp.transpose(mixer_in, (1, 2, 0))
    ws = jnp.transpose(shared_in)
    wt = jnp.transpose(step_in).reshape(n_short, heads, width)
    weights = (wm.size + ws.size + wt.size) * 2
    order = sum(layout, [])
    xg, send, aux = call(
        functools.partial(project_body, shared, len(pieces)),
        (
            jax.ShapeDtypeStruct((rows, width), BF16),
            jax.ShapeDtypeStruct((rows, sent), F32),
            jax.ShapeDtypeStruct((rows, sent - round_up(columns, LANES)), F32),
        ),
        (place, cos, *pieces, gain, wm, ws, wt),
        [IN_SMEM, ANYWHERE] + [IN_VMEM] * (len(pieces) + 4),
        flops=rows * weights,
        nbytes=20 * weights,
        name="project",
    )
    received = lax.ppermute(send, "short", other_core)
    keep = call(
        own_group_body,
        jax.ShapeDtypeStruct((rows, round_up(columns, LANES)), F32),
        (place, xg, wm),
        [IN_SMEM, IN_VMEM, IN_VMEM],
        flops=rows * weights,
        nbytes=weights // 2,
        name="own_group",
    )
    *parts, inv, step_raw = call(
        functools.partial(combine_body, width * n_short, order),
        part_shapes(n_wide, own_rows, used, 1)
        + (
            jax.ShapeDtypeStruct((rows, LANES), F32),
            jax.ShapeDtypeStruct((own_rows, LANES), F32),
        ),
        (keep, aux, received),
        [IN_VMEM] * 3,
        flops=4 * rows * sent,
        nbytes=8 * rows * sent,
        name="combine",
    )
    made = []

    def gate(after):
        made.append(
            call(
                gate_body,
                jax.ShapeDtypeStruct((rows, ff), F32),
                (xg, inv, gate_weight),
                [IN_VMEM] * 3,
                flops=2 * rows * width * ff,
                nbytes=2 * width * ff,
                name="gate",
            )
        )
        return made

    def up(after):
        made.extend(
            call(
                up_body,
                (jax.ShapeDtypeStruct((rows, ff), F32), jax.ShapeDtypeStruct((2, rows, ff), BF16)),
                (xg, inv, up_weight, made[0], after),
                [IN_VMEM] * 4 + [ANYWHERE],
                flops=2 * rows * width * ff,
                nbytes=2 * width * ff,
                name="up",
            )
        )
        return made[1:]

    features, layout = exchange(parts, n_wide, (gate, up), first=1)
    gate_own, up_own, ff_send = made
    features, ff_send = lax.optimization_barrier((features, ff_send))
    ff_received = lax.ppermute(ff_send, "short", other_core)
    out_shapes = part_shapes(n_wide, own_rows, piece)
    full_rows = round_up(own_rows, 8)
    parts = call(
        functools.partial(
            mixer_body,
            (columns, shared, round_up(columns, LANES), q_heads, kv_heads, heads, head_width),
            layout,
            len(out_shapes),
        ),
        out_shapes,
        (
            lengths,
            place,
            *features,
            step_raw,
            cos,
            sin,
            step_bias.reshape(1, heads),
            decay_rate.reshape(1, heads),
            skip_gain.reshape(1, heads),
            mixer_gain.reshape(1, heads * head_width),
            cached_keys[0],
            cached_values[0],
            state_cache.reshape(heads * head_width, states),
            up_own,
        ),
        [IN_SMEM] * 2 + [IN_VMEM] * (len(features) + 10) + [ANYWHERE],
        [
            pltpu.VMEM((n_wide, full_rows, used), F32),
            pltpu.VMEM((full_rows, n_wide * columns), F32),
            pltpu.VMEM((full_rows, n_wide * shared), F32),
            pltpu.VMEM((full_rows, n_wide * piece), F32),
            pltpu.VMEM((n_wide, full_rows, piece), F32),
        ],
        flops=4 * own_rows * state_cache.size,
        nbytes=6 * state_cache.size,
        name="mixers",
    )
    ff_out = []

    def down(after):
        ff_out.append(
            call(
                down_body,
                jax.ShapeDtypeStruct((rows, width), F32),
                (gate_own, up_own, ff_received, down_weight, after),
                [IN_VMEM] * 4 + [ANYWHERE],
                [pltpu.VMEM((rows, ff), BF16)],
                flops=2 * rows * width * ff,
                nbytes=2 * width * ff,
                name="down",
            )
        )
        return ff_out

    mine, layout, other = exchange(parts, n_wide, (down,), other_core=True)
    summed = call(
        functools.partial(output_body, layout, order),
        jax.ShapeDtypeStruct((n_wide, own_rows, width), BF16),
        (place, *mine, *other, mixer_out, ff_out[0]),
        [IN_SMEM] + [IN_VMEM] * (2 * len(mine) + 2),
        flops=4 * rows * width * piece,
        nbytes=4 * width * piece,
        name="output",
    )
    pieces = lax.all_to_all(summed, "wide", split_axis=0, concat_axis=0, tiled=True)
    total = tokens.astype(F32) + jnp.sum(pieces.astype(F32), axis=0)
    return total.astype(BF16)


def solution(mesh):
    in_specs = (
        P(("groups", "wide"), "short"),
        P("short"),
        P("short", None, "wide"),
        P("short", "wide"),
        P("short", None),
        P("short"),
        P("short"),
        P("short"),
        P(("groups", "wide"), None, "short"),
        P(("groups", "wide"), None, "short"),
        P(("groups", "wide")),
        P(("groups", "wide"), "short", None, None),
        P("short"),
        P(None, "wide", "short"),
        P("short", "wide"),
        P("short", "wide"),
        P("wide", "short"),
    )
    out_specs = P(("groups", "wide"), "short")
    return jax.shard_map(
        on_device, mesh=mesh, in_specs=in_specs, out_specs=out_specs, check_vma=False
    )
```
